1024 devices in a mesh: group: 8 (over y), expert: 32 (over z, core), rep: 4 (over x).
Axes of the slice: x: 4, y: 8, z: 16, core: 2. Of those that a mesh axis runs over, the one named last changes fastest.
Arguments:
- tokens: bfloat16 [2048, 4096], P(('group', 'expert')), may hold values from -6 to 6
- cotangent: bfloat16 [2048, 4096], P(('group', 'expert')), may hold values from -6 to 6
- router: bfloat16 [4096, 128], P(None, 'group'), may hold values from -0.09375 to 0.09375
- w_gate: bfloat16 [256, 4096, 512], P(('group', 'expert'), None, 'rep'), may hold values from -0.09375 to 0.09375
- w_up: bfloat16 [256, 4096, 512], P(('group', 'expert'), None, 'rep'), may hold values from -0.09375 to 0.09375
- w_down: bfloat16 [256, 512, 4096], P(('group', 'expert'), 'rep'), may hold values from -0.1875 to 0.1875
- group_picks: int32 [8, 32, 64, 2], P('group', 'expert'), may hold values from -1 to 15, as said below
Outputs:
- layer_out: bfloat16 [2048, 4096], P(('group', 'expert'), 'rep')
- input_grad: bfloat16 [2048, 4096], P(('group', 'expert'), 'rep')
The draws below stay inside these ranges and needn't reach their ends.
Inputs may be any that keep to these rules, and one draw needn't show every extreme that they name: group_picks[g, c, t] holds two different in-group experts that column token t of column c names in group g, or -1 twice where the token names none there. Every token names exactly 4 groups, and each group is named by exactly 32 tokens of every column. In one group and column an expert is named by at most 8 tokens; in every column some experts of every group are named by exactly 8.
All inputs are finite; a program needn't handle non-finite values.
Results may differ from the reference program's by a relative error of at most 0.015.
Values may be sent and summed in bfloat16 or wider, within the bound.
A program may use at most 32 MiB of HBM per device.

```python
import jax
import jax.numpy as jnp
from jax import lax

D = 4096
H = 1024
TOK_DEV = 8
EXP_GROUP = 16
EXPERTS = 128
HOT = 4
CAP = 8
COL_TOK = 64
TOKENS = 2048
N_GROUP = 8
N_EXPERT = 32
N_REP = 4


def permute_many(seed_key, number, length):
    return jax.vmap(lambda seed_one: jax.random.permutation(seed_one, length))(jax.random.split(seed_key, number))


def draw_group_picks(key, part):
    key = jax.random.fold_in(key, 7)
    subkeys = jax.random.split(key, 5)
    col_tokens = N_GROUP * TOK_DEV
    half_picks = 4 * TOK_DEV
    position = permute_many(subkeys[0], N_EXPERT, col_tokens).astype(jnp.int32)
    relabel = permute_many(subkeys[1], N_EXPERT, N_GROUP).astype(jnp.int32)
    first_rank = permute_many(subkeys[2], N_EXPERT * N_GROUP, half_picks).reshape(N_EXPERT, N_GROUP, half_picks).astype(jnp.int32)
    second_rank = permute_many(subkeys[3], N_EXPERT * N_GROUP, half_picks).reshape(N_EXPERT, N_GROUP, half_picks).astype(jnp.int32)
    hotness = permute_many(subkeys[4], N_GROUP, EXP_GROUP).astype(jnp.int32)
    offsets = jnp.arange(4, dtype=jnp.int32)
    slot_group = (position[:, :, None] % N_GROUP + offsets) % N_GROUP
    column_ids = jnp.arange(N_EXPERT, dtype=jnp.int32)[:, None, None]
    group_label = relabel[column_ids, slot_group]
    slot_rank = 4 * (position[:, :, None] // N_GROUP) + offsets
    first_pos = first_rank[column_ids, group_label, slot_rank]
    second_pos = second_rank[column_ids, group_label, slot_rank]
    hot_slot = first_pos // CAP
    cold_slot = HOT + second_pos * (EXP_GROUP - HOT) // half_picks
    picked = jnp.stack([hotness[group_label, hot_slot], hotness[group_label, cold_slot]], axis=-1)
    token_ids = jnp.arange(col_tokens, dtype=jnp.int32)[None, :, None]
    result = jnp.full((N_GROUP, N_EXPERT, col_tokens, 2), -1, dtype=jnp.int32)
    result = result.at[group_label, column_ids, token_ids].set(picked)
    return result


def level_of(own_key, shape, shards, least, top_value):
    def one(dim, shards_of):
        steps = jax.random.uniform(jax.random.fold_in(jax.random.fold_in(own_key, 6), dim), (shards_of,), jnp.float32, least / len(shards), top_value / len(shards))
        return jnp.repeat(jnp.exp(steps), shape[dim] // shards_of).reshape((-1,) + (1,) * (len(shape) - dim - 1))

    level = one(*shards[0])
    for cut in shards[1:]:
        level = level * one(*cut)
    return level


def noise(own_key, shape, scale, bound, cuts=(), held_as=jnp.bfloat16):
    values = jax.random.normal(own_key, shape, jnp.float32) * scale
    if len(cuts) > 0:
        values = level_of(own_key, shape, cuts, -0.22, 0.18) * values
    return jnp.clip(values, min=-bound, max=bound).astype(held_as)


def setup_inputs(seed: int = 0) -> dict:
    keys = jax.random.split(jax.random.key(seed), 8)
    tokens = noise(keys[0], (TOKENS, D), 1.0, 6.0, ((0, 256),))
    cotangent = noise(keys[1], (TOKENS, D), 1.0, 6.0, ((0, 256),))
    router = noise(keys[2], (D, EXPERTS), D ** -0.5, 0.09375, ((1, 8),))
    w_gate = noise(keys[3], (EXPERTS * 2, D, H // 2), D ** -0.5, 0.09375, ((0, 256), (2, 4)))
    w_up = noise(keys[4], (EXPERTS * 2, D, H // 2), D ** -0.5, 0.09375, ((0, 256), (2, 4)))
    w_down = noise(keys[5], (EXPERTS * 2, H // 2, D), H ** -0.5, 0.1875, ((0, 256), (1, 4)))
    group_picks = draw_group_picks(jax.random.fold_in(keys[7], 71), 0)
    return {"tokens": tokens, "cotangent": cotangent, "router": router, "w_gate": w_gate, "w_up": w_up, "w_down": w_down, "group_picks": group_picks}


route_scale = 2.5

def sectioned_sum(parts):
    first = lax.optimization_barrier(parts.astype(jnp.bfloat16)).astype(jnp.float32)
    first = lax.optimization_barrier(jnp.sum(first.reshape((2, N_REP) + parts.shape[1:]), axis=1))
    second = lax.optimization_barrier(first.astype(jnp.bfloat16)).astype(jnp.float32)
    return lax.optimization_barrier(jnp.sum(second, axis=0))

def expert_terms(expert_rows, expert_grads, gate_w, up_w, down_w):
    largest_score = lax.Precision.HIGHEST
    blocks = 2 * N_REP
    block_size = H // blocks
    row_count = expert_rows.shape[0]
    gate_value = jnp.dot(expert_rows, gate_w, preferred_element_type=jnp.float32)
    up_value = jnp.dot(expert_rows, up_w, preferred_element_type=jnp.float32)
    gate_sig = jax.nn.sigmoid(gate_value)
    gate_act = gate_value * gate_sig
    hidden = (gate_act * up_value).astype(jnp.bfloat16)
    grad_hidden = jnp.dot(expert_grads, down_w.T, preferred_element_type=jnp.float32)
    grad_gate = (grad_hidden * up_value * gate_sig * (1.0 + gate_value * (1.0 - gate_sig))).astype(jnp.bfloat16)
    grad_up = (grad_hidden * gate_act).astype(jnp.bfloat16)
    hidden_bias_grad = hidden.astype(jnp.float32).reshape(row_count, blocks, block_size)
    down_bias_grad = down_w.astype(jnp.float32).reshape(blocks, block_size, D)
    gate_b = gate_w.astype(jnp.float32).reshape(D, blocks, block_size)
    up_b = up_w.astype(jnp.float32).reshape(D, blocks, block_size)
    output_pieces = jnp.einsum('jvn,vnp->vjp', hidden_bias_grad, down_bias_grad, precision=largest_score)
    grad_parts = jnp.einsum('rbk,dbk->brd', grad_gate.astype(jnp.float32).reshape(row_count, blocks, block_size), gate_b, precision=largest_score)
    grad_parts = grad_parts + jnp.einsum('rbk,dbk->brd', grad_up.astype(jnp.float32).reshape(row_count, blocks, block_size), up_b, precision=largest_score)
    dot_parts = jnp.einsum('rbk,rbk->br', grad_hidden.reshape(row_count, blocks, block_size), hidden_bias_grad, precision=largest_score)
    return (sectioned_sum(output_pieces), sectioned_sum(grad_parts), sectioned_sum(dot_parts))

def reference(tokens, cotangent, router, w_gate, w_up, w_down, group_picks):
    largest_score = lax.Precision.HIGHEST
    column_x = tokens.reshape(N_GROUP, N_EXPERT, TOK_DEV, D).transpose(1, 0, 2, 3).reshape(N_EXPERT, COL_TOK, D)
    column_dy = cotangent.reshape(N_GROUP, N_EXPERT, TOK_DEV, D).transpose(1, 0, 2, 3).reshape(N_EXPERT, COL_TOK, D)
    expert_ids = jnp.arange(EXP_GROUP, dtype=jnp.int32)
    places = jnp.arange(CAP, dtype=jnp.int32)
    positions = jnp.arange(COL_TOK, dtype=jnp.int32)

    def group_step(carry, group_index):
        pick_list = lax.dynamic_index_in_dim(group_picks, group_index, 0, keepdims=False)
        onehot = lax.optimization_barrier(jnp.sum((pick_list[..., None] == expert_ids).astype(jnp.int32), axis=2))
        prior_value = jnp.cumsum(onehot, axis=1) - onehot
        select = (onehot.transpose(0, 2, 1)[:, :, None, :] == 1) & (prior_value.transpose(0, 2, 1)[:, :, None, :] == places[None, None, :, None])
        token_index = lax.optimization_barrier(jnp.sum(select.astype(jnp.int32) * positions, axis=3))
        filled = jnp.any(select, axis=3)
        take_rows = jax.vmap(lambda source_rows, source_index: source_rows[source_index])
        slot_x = jnp.where(filled[..., None], take_rows(column_x, token_index), 0).astype(jnp.bfloat16)
        slot_dy = jnp.where(filled[..., None], take_rows(column_dy, token_index), 0).astype(jnp.bfloat16)

        def one_expert(local_index):
            expert = group_index * EXP_GROUP + local_index
            expert_rows = lax.dynamic_index_in_dim(slot_x, local_index, 1, keepdims=False).reshape(N_EXPERT * CAP, D)
            expert_grads = lax.dynamic_index_in_dim(slot_dy, local_index, 1, keepdims=False).reshape(N_EXPERT * CAP, D)
            gate_pair = lax.dynamic_slice_in_dim(w_gate, 2 * expert, 2, 0)
            up_pair = lax.dynamic_slice_in_dim(w_up, 2 * expert, 2, 0)
            down_pair = lax.dynamic_slice_in_dim(w_down, 2 * expert, 2, 0)
            gate_w = jnp.concatenate([gate_pair[0], gate_pair[1]], axis=1)
            up_w = jnp.concatenate([up_pair[0], up_pair[1]], axis=1)
            down_w = jnp.concatenate([down_pair[0], down_pair[1]], axis=0)
            return expert_terms(expert_rows, expert_grads, gate_w, up_w, down_w)
        expert_out, expert_grad, expert_dot = lax.map(one_expert, expert_ids)
        expert_out = expert_out.reshape(EXP_GROUP, N_EXPERT, CAP, D)
        expert_grad = expert_grad.reshape(EXP_GROUP, N_EXPERT, CAP, D)
        expert_dot = expert_dot.reshape(EXP_GROUP, N_EXPERT, CAP)
        router_group = lax.dynamic_slice_in_dim(router, group_index * EXP_GROUP, EXP_GROUP, 1)
        logits = jnp.dot(column_x.reshape(N_EXPERT * COL_TOK, D), router_group, preferred_element_type=jnp.float32)
        expert_scores = jax.nn.sigmoid(logits).reshape(N_EXPERT, COL_TOK, EXP_GROUP)
        select_f = select.astype(jnp.float32)
        weighted = select_f * expert_scores.transpose(0, 2, 1)[:, :, None, :]
        mixed = jnp.einsum('cekt,eckd->ctd', weighted, expert_out, precision=largest_score)
        grad_mix = jnp.einsum('cekt,eckd->ctd', weighted, expert_grad, precision=largest_score)
        pick_dot = jnp.einsum('cekt,eck->cte', select_f, expert_dot, precision=largest_score)
        chosen = onehot.astype(jnp.float32)
        gate_slope = expert_scores * (1.0 - expert_scores) * chosen
        router_f = router_group.astype(jnp.float32)
        grad_mix = grad_mix + jnp.einsum('cte,de->ctd', gate_slope * pick_dot, router_f, precision=largest_score)
        gate_grad = jnp.einsum('cte,de->ctd', gate_slope, router_f, precision=largest_score)
        gate_total = lax.optimization_barrier(jnp.sum(expert_scores * chosen, axis=2))
        dot_total = lax.optimization_barrier(jnp.sum(expert_scores * chosen * pick_dot, axis=2))
        mix_sum, grad_sum, slope_sum, gate_weight_total, dot_sum = carry
        return ((mix_sum + mixed, grad_sum + grad_mix, slope_sum + gate_grad, gate_weight_total + gate_total, dot_sum + dot_total), None)
    wide_zero = jnp.zeros((N_EXPERT, COL_TOK, D), jnp.float32)
    narrow_zero = jnp.zeros((N_EXPERT, COL_TOK), jnp.float32)
    start = (wide_zero, wide_zero, wide_zero, narrow_zero, narrow_zero)
    totals, _ = lax.scan(group_step, start, jnp.arange(N_GROUP, dtype=jnp.int32))
    mix_sum, grad_sum, slope_sum, gate_weight_total, dot_sum = totals
    factor = route_scale / gate_weight_total
    layer_out = (mix_sum * factor[..., None]).astype(jnp.bfloat16)
    input_grad = (grad_sum * factor[..., None] - slope_sum * (factor * dot_sum / gate_weight_total)[..., None]).astype(jnp.bfloat16)

    def to_rows(column_major):
        return column_major.reshape(N_EXPERT, N_GROUP, TOK_DEV, D).transpose(1, 0, 2, 3).reshape(TOKENS, D)
    return (to_rows(layer_out), to_rows(input_grad))
```

```python
import functools

import jax
import jax.numpy as jnp
from jax import lax
from jax.experimental import pallas as pl
from jax.experimental.pallas import tpu as pltpu
from jax.sharding import PartitionSpec as P

MESH = pl.DeviceIdType.MESH
F32 = jnp.float32
BF16 = jnp.bfloat16
route_scale = 2.5
NT = (((1,), (1,)), ((), ()))


def rcopy(src, dst, send, recv, device):
    return pltpu.make_async_remote_copy(
        src_ref=src, dst_ref=dst, send_sem=send, recv_sem=recv, device_id=device, device_id_type=MESH
    )


def kernel(
    ny, nz, nx, chunks,
    tok_ref, cot_ref, router_ref, wg_ref, wu_ref, wd_ref, picks_ref,
    out_ref, grad_ref,
    wgu, wd, col, rt, slots, xr, pt, prcv, sa, ra, sb, rb, zs, ret, mg, mgr, st, hs, lg, pd, sel_s, wt,
    w_sem,
    yt_s, yt_r, yr_s, yr_r, ym_s, ym_r, ys_s, ys_r,
    zf_s, zf_r, zr_s, zr_r,
    lg_s, lg_r, pd_s, pd_r,
    xa_s, xa_r, xd_s, xd_r, pc_s, pc_r, pr_s, pr_r, ra_s, ra_r, rb_s, rb_r,
):
    y = lax.axis_index("group")
    e = lax.axis_index("expert")
    x = lax.axis_index("rep")
    z = e // 2
    core = e % 2
    other = 1 - core
    width = tok_ref.shape[1] // nx
    groups = nz // chunks
    half = chunks // 2
    lanes = ny * 16
    right, left = (x + 1) % nx, (x + nx - 1) % nx
    across = (x + 2) % nx

    def at_y(i):
        return {"group": i}

    def at_z(i):
        return {"expert": i * 2 + core}

    def at_x(i):
        return {"rep": i}

    partner = {"expert": z * 2 + other}

    def offset(p):
        g = p // 2
        m = (g + 1) // 2
        sign = 2 * (g % 2) - 1
        return (p % 2) * (-sign * (nz // 2 - m)) + (1 - p % 2) * (sign * m)

    load_gate = pltpu.make_async_copy(wg_ref.at[0], wgu.at[:, 0:128], w_sem.at[0])
    load_up = pltpu.make_async_copy(wu_ref.at[0], wgu.at[:, 128:256], w_sem.at[1])
    load_down = pltpu.make_async_copy(wd_ref.at[0], wd, w_sem.at[2])
    load_gate.start()
    load_up.start()
    load_down.start()

    barrier = pltpu.get_barrier_semaphore()
    for d in range(1, ny):
        pl.semaphore_signal(barrier, inc=1, device_id=at_y((y + d) % ny), device_id_type=MESH)
    for d in range(1, nx):
        pl.semaphore_signal(barrier, inc=1, device_id=at_x((x + d) % nx), device_id_type=MESH)
    pl.semaphore_signal(barrier, inc=1, device_id=partner, device_id_type=MESH)

    def greet(d, carry):
        pl.semaphore_signal(barrier, inc=1, device_id=at_z((z + d) % nz), device_id_type=MESH)
        return carry

    lax.fori_loop(1, nz, greet, 0)
    quarter = pl.ds(pl.multiple_of(x * width, 128), width)
    col[y] = jnp.concatenate(
        [tok_ref[:, quarter].astype(F32), cot_ref[:, quarter].astype(F32)], axis=0
    ).astype(BF16)
    rt[y] = router_ref[:, quarter]
    pl.semaphore_wait(barrier, ny - 1 + nx - 1 + 1 + nz - 1)

    for d in range(1, ny):
        there = (y + d) % ny
        rcopy(col.at[y], col.at[y], yt_s.at[d], yt_r.at[d], at_y(there)).start()
    for d in range(1, ny):
        there = (y + d) % ny
        rcopy(rt.at[y], rt.at[y], yr_s.at[d], yr_r.at[d], at_y(there)).start()

    picks = picks_ref[...]
    tokens_here = ny * 8
    ids = lax.broadcasted_iota(jnp.int32, (nz, tokens_here), 0)
    onehot = ((picks[0:1, :] == ids) | (picks[1:2, :] == ids)).astype(F32).astype(BF16)
    t_row = lax.broadcasted_iota(jnp.int32, (tokens_here, lanes), 0)
    q_col = lax.broadcasted_iota(jnp.int32, (tokens_here, lanes), 1)
    t_col = (q_col // 16) * 8 + q_col % 8
    spread = (t_row == t_col).astype(F32).astype(BF16)
    before = (t_row < t_col).astype(F32).astype(BF16)
    onehot_q = jnp.dot(onehot, spread, preferred_element_type=F32)
    prior = jnp.dot(onehot, before, preferred_element_type=F32)
    shape3 = (nz, 16, lanes)
    row = lax.broadcasted_iota(jnp.int32, shape3, 1)
    lane = lax.broadcasted_iota(jnp.int32, shape3, 2)
    same_kind = (row // 8) == ((lane // 8) % 2)
    slot = (row % 8).astype(F32)
    picked = jnp.where(
        same_kind & (jnp.broadcast_to(prior[:, None, :], shape3) == slot),
        jnp.broadcast_to(onehot_q[:, None, :], shape3),
        0.0,
    )
    sel_s[...] = picked

    for d in range(1, ny):
        rcopy(col.at[y], col.at[(y + ny - d) % ny], yt_s.at[d], yt_r.at[d], at_y(y)).wait_recv()
    column = col[...].reshape(lanes, width)
    slots[...] = (
        jnp.dot(picked.reshape(nz * 16, lanes).astype(BF16), column, preferred_element_type=F32)
        .astype(BF16)
        .reshape(nz, 16, width)
    )

    def z_forward(p):
        there = (z - offset(p) + nz) % nz
        return rcopy(slots.at[there], xr.at[x, p, core], zf_s.at[p], zf_r.at[p], at_z(there))

    def z_send(p, carry):
        z_forward(p).start()
        return carry

    lax.fori_loop(1, nz, z_send, 0)
    xr[x, 0, core] = slots[z]

    logits = lax.dot_general(rt[y], column, NT, preferred_element_type=F32)
    lg[x] = logits
    for d in range(1, nx):
        rcopy(lg.at[x], lg.at[x], lg_s.at[d], lg_r.at[d], at_x((x + d) % nx)).start()

    def part(g):
        return pl.ds(g * chunks, chunks)

    def first(g):
        return pl.ds(g * chunks, half)

    def second(g):
        return pl.ds(g * chunks + half, half)

    def to_side(q, g, side, device):
        block = xr.at[q, part(g), core]
        return rcopy(block, block, xa_s.at[g, side], xa_r.at[g, side], device)

    def onward(q, places, g, side, device):
        block = xr.at[q, places, core]
        return rcopy(block, block, xd_s.at[g, side], xd_r.at[g, side], device)

    def to_partner(q, g):
        block = xr.at[q, part(g), core]
        return rcopy(block, block, pc_s.at[g, q], pc_r.at[g, q], partner)

    def from_partner(q, g):
        block = xr.at[q, part(g), other]
        return rcopy(block, block, pc_s.at[g, q], pc_r.at[g, q], partner)

    def parts_to_partner(g):
        return rcopy(pt.at[:, part(g), other], prcv.at[:, part(g)], pr_s.at[g], pr_r.at[g], partner)

    def pair_sum(q, places):
        return pt[q, places, core].astype(F32) + prcv[q, places].astype(F32)

    def sum_across(places, g, side, device):
        return rcopy(sa.at[places], ra.at[places], ra_s.at[g, side], ra_r.at[g, side], device)

    def sum_side(g, side, device):
        return rcopy(sb.at[side, part(g)], rb.at[side, part(g)], rb_s.at[g, side], rb_r.at[g, side], device)

    def z_back(p):
        there = (z + offset(p) + nz) % nz
        return rcopy(zs.at[p], ret.at[z], zr_s.at[p], zr_r.at[p], at_z(there))

    def stage_arrive(g):
        def wait_one(p, carry):
            z_forward(p).wait_recv()
            return carry

        lax.fori_loop(jnp.maximum(g * chunks, 1), (g + 1) * chunks, wait_one, 0)
        to_side(x, g, 0, at_x(right)).start()
        to_side(x, g, 1, at_x(left)).start()
        to_partner(x, g).start()

    def stage_sides(g):
        to_side(left, g, 0, at_x(right)).wait_recv()
        onward(left, first(g), g, 0, at_x(right)).start()
        to_partner(left, g).start()
        to_side(right, g, 1, at_x(left)).wait_recv()
        onward(right, second(g), g, 1, at_x(left)).start()
        to_partner(right, g).start()

    def stage_across(g):
        onward(across, first(g), g, 0, at_x(right)).wait_recv()
        onward(across, second(g), g, 1, at_x(left)).wait_recv()
        to_partner(across, g).start()

    def stage_compute(g):
        for q in range(nx):
            from_partner(q, g).wait_recv()
        rows = chunks * 2
        gate_up = jnp.zeros((rows * 16, 256), F32)
        grad_hidden = jnp.zeros((rows * 16, 128), F32)
        for q in range(nx):
            block = xr[q, part(g)].reshape(rows * 16, width)
            depth = slice(q * width, (q + 1) * width)
            gate_up = gate_up + jnp.dot(block, wgu[depth, :], preferred_element_type=F32)
            grad_hidden = grad_hidden + lax.dot_general(
                block, wd[:, depth], NT, preferred_element_type=F32
            )
        gate_up = gate_up.reshape(rows, 16, 256)[:, 0:8, :].reshape(rows * 8, 256)
        grad_hidden = grad_hidden.reshape(rows, 16, 128)[:, 8:16, :].reshape(rows * 8, 128)
        gate, up = gate_up[:, 0:128], gate_up[:, 128:256]
        sig = jax.nn.sigmoid(gate)
        act = gate * sig
        hidden = (act * up).astype(BF16)
        both = jnp.concatenate(
            [grad_hidden * up * sig * (1.0 + gate * (1.0 - sig)), grad_hidden * act], axis=1
        ).astype(BF16)
        for q in range(nx):
            depth = slice(q * width, (q + 1) * width)
            out = jnp.dot(hidden, wd[:, depth], preferred_element_type=F32)
            grad = lax.dot_general(both, wgu[depth, :], NT, preferred_element_type=F32)
            joined = jnp.concatenate(
                [out.reshape(rows, 8, width), grad.reshape(rows, 8, width)], axis=1
            ).astype(BF16)
            pt[q, part(g)] = joined.reshape(chunks, 2, 16, width)
        parts_to_partner(g).start()

    def stage_pair(g):
        parts_to_partner(g).wait_recv()
        sa[part(g)] = pair_sum(across, part(g)).astype(BF16)
        sum_across(first(g), g, 0, at_x(right)).start()
        sum_across(second(g), g, 1, at_x(left)).start()

    def stage_add(g):
        sum_across(first(g), g, 0, at_x(right)).wait_recv()
        sum_across(second(g), g, 1, at_x(left)).wait_recv()
        sb[0, first(g)] = (pair_sum(right, first(g)) + ra[first(g)].astype(F32)).astype(BF16)
        sb[0, second(g)] = pair_sum(right, second(g)).astype(BF16)
        sum_side(g, 0, at_x(right)).start()
        sb[1, first(g)] = pair_sum(left, first(g)).astype(BF16)
        sb[1, second(g)] = (pair_sum(left, second(g)) + ra[second(g)].astype(F32)).astype(BF16)
        sum_side(g, 1, at_x(left)).start()

    def stage_return(g):
        sum_side(g, 0, at_x(right)).wait_recv()
        sum_side(g, 1, at_x(left)).wait_recv()
        zs[part(g)] = (
            pair_sum(x, part(g)) + rb[0, part(g)].astype(F32) + rb[1, part(g)].astype(F32)
        ).astype(BF16)

        def send_one(p, carry):
            z_back(p).start()
            return carry

        lax.fori_loop(jnp.maximum(g * chunks, 1), (g + 1) * chunks, send_one, 0)

    load_gate.wait()
    load_up.wait()
    load_down.wait()

    stages = (
        stage_arrive, stage_sides, stage_across, stage_compute, stage_pair, stage_add, stage_return
    )

    def step(it, carry):
        for lag in range(len(stages) - 1, -1, -1):
            g = it - lag

            @pl.when((g >= 0) & (g < groups))
            def _(stage=stages[lag], g=g):
                stage(g)

        return carry

    lax.fori_loop(0, groups + len(stages) - 1, step, 0)

    for d in range(1, nx):
        rcopy(lg.at[x], lg.at[(x + nx - d) % nx], lg_s.at[d], lg_r.at[d], at_x(x)).wait_recv()
    score = jax.nn.sigmoid((lg[0] + lg[1]) + (lg[2] + lg[3]))
    lane2 = lax.broadcasted_iota(jnp.int32, (nz, lanes), 1)
    token_lane = (lane2 // 8) % 2 == 0
    score = jnp.where(token_lane, score, pltpu.roll(score, 8, 1))
    weighted = sel_s[...] * jnp.broadcast_to(score[:, None, :], shape3)
    weighted = jnp.transpose(weighted.reshape(nz * 16, lanes))
    high = weighted.astype(BF16)
    wt[0] = high
    wt[1] = (weighted - high.astype(F32)).astype(BF16)

    ret[z] = zs[0]

    def wait_back(p, carry):
        there = (z - offset(p) + nz) % nz
        rcopy(zs.at[p], ret.at[there], zr_s.at[p], zr_r.at[p], at_z(z)).wait_recv()
        return carry

    lax.fori_loop(1, nz, wait_back, 0)
    back = ret[...].reshape(nz * 16, width)
    cross = lax.dot_general(back, col[...].reshape(lanes, width), NT, preferred_element_type=F32)
    cross = cross.reshape(shape3)[:, 0:8, :] * sel_s[:, 8:16, :]
    pd[x] = jnp.sum(cross, axis=1)
    for d in range(1, nx):
        rcopy(pd.at[x], pd.at[x], pd_s.at[d], pd_r.at[d], at_x((x + d) % nx)).start()
    mixed = jnp.dot(wt[0], back, preferred_element_type=F32) + jnp.dot(
        wt[1], back, preferred_element_type=F32
    )
    mg[...] = mixed.astype(BF16).reshape(ny, 16, width)
    for d in range(1, ny):
        there = (y + d) % ny
        rcopy(mg.at[there], mgr.at[y], ym_s.at[d], ym_r.at[d], at_y(there)).start()
    mgr[y] = mg[y]
    for d in range(1, nx):
        rcopy(pd.at[x], pd.at[(x + nx - d) % nx], pd_s.at[d], pd_r.at[d], at_x(x)).wait_recv()
    table = jnp.where(token_lane, score * onehot_q, (pd[0] + pd[1]) + (pd[2] + pd[3]))
    table = jnp.concatenate([table, jnp.zeros((128 - nz, lanes), F32)], axis=0)
    st[...] = jnp.transpose(table).reshape(ny, 16, 128)
    for d in range(1, ny):
        there = (y + d) % ny
        rcopy(st.at[there], hs.at[y], ys_s.at[d], ys_r.at[d], at_y(there)).start()
    hs[y] = st[y]

    for d in range(1, ny):
        there = (y + ny - d) % ny
        rcopy(rt.at[there], rt.at[there], yr_s.at[d], yr_r.at[d], at_y(y)).wait_recv()
        rcopy(mg.at[there], mgr.at[there], ym_s.at[d], ym_r.at[d], at_y(y)).wait_recv()
        rcopy(st.at[there], hs.at[there], ys_s.at[d], ys_r.at[d], at_y(y)).wait_recv()
    total = mgr[0].astype(F32)
    terms = hs[0]
    for g in range(1, ny):
        total = total + mgr[g].astype(F32)
        terms = terms + pltpu.roll(hs[g], g * nz, 1)
    s, dots = terms[0:8], terms[8:16]
    slope = s * (1.0 - s)
    dot_slope = slope * dots
    slope_high = slope.astype(BF16).astype(F32)
    dot_high = dot_slope.astype(BF16).astype(F32)
    factors = jnp.concatenate(
        [slope_high, slope - slope_high, dot_high, dot_slope - dot_high], axis=0
    ).astype(BF16)
    experts = ny * nz
    by_router = jnp.dot(
        factors[:, 0:experts], rt[...].reshape(experts, width), preferred_element_type=F32
    )
    slope_sum = by_router[0:8] + by_router[8:16]
    grad_sum = total[8:16] + (by_router[16:24] + by_router[24:32])
    gate_sum = jnp.sum(s, axis=1, keepdims=True)
    dot_sum = jnp.sum(s * dots, axis=1, keepdims=True)
    factor = route_scale / gate_sum
    out_ref[...] = (total[0:8] * factor).astype(BF16)
    grad_ref[...] = (grad_sum * factor - slope_sum * (factor * dot_sum / gate_sum)).astype(BF16)

    for d in range(1, ny):
        rcopy(col.at[y], col.at[y], yt_s.at[d], yt_r.at[d], at_y(y)).wait_send()
        rcopy(rt.at[y], rt.at[y], yr_s.at[d], yr_r.at[d], at_y(y)).wait_send()
        rcopy(mg.at[y], mgr.at[y], ym_s.at[d], ym_r.at[d], at_y(y)).wait_send()
        rcopy(st.at[y], hs.at[y], ys_s.at[d], ys_r.at[d], at_y(y)).wait_send()
    for d in range(1, nx):
        rcopy(lg.at[x], lg.at[x], lg_s.at[d], lg_r.at[d], at_x(x)).wait_send()
        rcopy(pd.at[x], pd.at[x], pd_s.at[d], pd_r.at[d], at_x(x)).wait_send()

    def sent_z(p, carry):
        z_forward(p).wait_send()
        z_back(p).wait_send()
        return carry

    lax.fori_loop(1, nz, sent_z, 0)

    def sent_group(g, carry):
        to_side(x, g, 0, at_x(right)).wait_send()
        to_side(x, g, 1, at_x(left)).wait_send()
        onward(left, first(g), g, 0, at_x(right)).wait_send()
        onward(right, second(g), g, 1, at_x(left)).wait_send()
        for q in range(nx):
            to_partner(q, g).wait_send()
        parts_to_partner(g).wait_send()
        sum_across(first(g), g, 0, at_x(right)).wait_send()
        sum_across(second(g), g, 1, at_x(left)).wait_send()
        sum_side(g, 0, at_x(right)).wait_send()
        sum_side(g, 1, at_x(left)).wait_send()
        return carry

    lax.fori_loop(0, groups, sent_group, 0)


def on_device(chunks, tokens, cotangent, router, w_gate, w_up, w_down, group_picks):
    ny = lax.axis_size("group")
    nz = lax.axis_size("expert") // 2
    nx = lax.axis_size("rep")
    width = tokens.shape[1] // nx
    groups = nz // chunks
    lanes = ny * 16
    dma = pltpu.SemaphoreType.DMA
    vmem = pl.BlockSpec(memory_space=pltpu.VMEM)
    hbm = pl.BlockSpec(memory_space=pl.ANY)
    result = jax.ShapeDtypeStruct((tokens.shape[0], width), BF16)
    return pl.pallas_call(
        functools.partial(kernel, ny, nz, nx, chunks),
        out_shape=(result, result),
        in_specs=[vmem, vmem, vmem, hbm, hbm, hbm, vmem],
        out_specs=(vmem, vmem),
        scratch_shapes=[
            pltpu.VMEM((nx * width, 256), BF16),
            pltpu.VMEM((128, nx * width), BF16),
            pltpu.VMEM((ny, 16, width), BF16),
            pltpu.VMEM((ny, nz, width), BF16),
            pltpu.VMEM((nz, 16, width), BF16),
            pltpu.VMEM((nx, nz, 2, 16, width), BF16),
            pltpu.VMEM((nx, nz, 2, 16, width), BF16),
            pltpu.VMEM((nx, nz, 16, width), BF16),
            pltpu.VMEM((nz, 16, width), BF16),
            pltpu.VMEM((nz, 16, width), BF16),
            pltpu.VMEM((2, nz, 16, width), BF16),
            pltpu.VMEM((2, nz, 16, width), BF16),
            pltpu.VMEM((nz, 16, width), BF16),
            pltpu.VMEM((nz, 16, width), BF16),
            pltpu.VMEM((ny, 16, width), BF16),
            pltpu.VMEM((ny, 16, width), BF16),
            pltpu.VMEM((ny, 16, 128), F32),
            pltpu.VMEM((ny, 16, 128), F32),
            pltpu.VMEM((nx, nz, lanes), F32),
            pltpu.VMEM((nx, nz, lanes), F32),
            pltpu.VMEM((nz, 16, lanes), F32),
            pltpu.VMEM((2, lanes, nz * 16), BF16),
            dma((3,)),
        ]
        + [dma((ny,))] * 8
        + [dma((nz,))] * 4
        + [dma((nx,))] * 4
        + [dma((groups, 2))] * 4
        + [dma((groups, nx))] * 2
        + [dma((groups,))] * 2
        + [dma((groups, 2))] * 4,
        compiler_params=pltpu.CompilerParams(
            collective_id=0, has_side_effects=True, vmem_limit_bytes=56 * 1024 * 1024
        ),
        cost_estimate=pl.CostEstimate(
            flops=3 * 1024 * 1024 * 1024, bytes_accessed=4 * 1024 * 1024, transcendentals=32768
        ),
    )(tokens, cotangent, router.T, w_gate, w_up, w_down, group_picks[0, 0].T)


def solution(mesh):
    return jax.shard_map(
        functools.partial(on_device, 4),
        mesh=mesh,
        in_specs=(
            P(("group", "expert"), None),
            P(("group", "expert"), None),
            P(None, "group"),
            P(("group", "expert"), None, "rep"),
            P(("group", "expert"), None, "rep"),
            P(("group", "expert"), "rep", None),
            P("group", "expert", None, None),
        ),
        out_specs=(P(("group", "expert"), "rep"), P(("group", "expert"), "rep")),
        check_vma=False,
    )
```

```python
import functools

import jax
import jax.numpy as jnp
from jax import lax
from jax.experimental import pallas as pl
from jax.experimental.pallas import tpu as pltpu
from jax.sharding import PartitionSpec as P

MESH = pl.DeviceIdType.MESH
F32 = jnp.float32
BF16 = jnp.bfloat16
route_scale = 2.5
NT = (((1,), (1,)), ((), ()))


def rcopy(src, dst, send, recv, device):
    return pltpu.make_async_remote_copy(
        src_ref=src, dst_ref=dst, send_sem=send, recv_sem=recv, device_id=device, device_id_type=MESH
    )


def kernel(
    ny, nz, nx, chunks, window,
    tok_ref, cot_ref, router_ref, wg_ref, wu_ref, wd_ref, picks_ref,
    out_ref, grad_ref,
    wgu, wd, wgu_t, wd_t, col, rt, slots, xr, pt, prcv, sb, rb, zs, ret, mg, mgr, st, hs, lg, pd, sel_s, wt,
    w_sem,
    yt_s, yt_r, yr_s, yr_r, ym_s, ym_r, ys_s, ys_r,
    zf_s, zf_r, zr_s, zr_r,
    lg_s, lg_r, pd_s, pd_r,
    xa_s, xa_r, pc_s, pc_r, pr_s, pr_r, rb_s, rb_r,
):
    y = lax.axis_index("group")
    e = lax.axis_index("expert")
    x = lax.axis_index("rep")
    z = e // 2
    core = e % 2
    other = 1 - core
    width = tok_ref.shape[1] // nx
    groups = nz // chunks
    lanes = ny * 16

    def at_y(i):
        return (i, e, x)

    def at_z(i):
        return (y, i * 2 + core, x)

    def at_x(i):
        return (y, e, i)

    partner = (y, z * 2 + other, x)

    def offset(p):
        g = p // 2
        m = (g + 1) // 2
        sign = 2 * (g % 2) - 1
        return (p % 2) * (-sign * (nz // 2 - m)) + (1 - p % 2) * (sign * m)

    load_gate = pltpu.make_async_copy(wg_ref.at[0], wgu.at[:, 0:128], w_sem.at[0])
    load_up = pltpu.make_async_copy(wu_ref.at[0], wgu.at[:, 128:256], w_sem.at[1])
    load_down = pltpu.make_async_copy(wd_ref.at[0], wd, w_sem.at[2])
    load_gate.start()
    load_up.start()
    load_down.start()

    barrier = pltpu.get_barrier_semaphore()
    for d in range(1, ny):
        pl.semaphore_signal(barrier, inc=1, device_id=at_y((y + d) % ny), device_id_type=MESH)
    for d in range(1, nx):
        pl.semaphore_signal(barrier, inc=1, device_id=at_x((x + d) % nx), device_id_type=MESH)
    pl.semaphore_signal(barrier, inc=1, device_id=partner, device_id_type=MESH)

    def greet(d, carry):
        pl.semaphore_signal(barrier, inc=1, device_id=at_z((z + d) % nz), device_id_type=MESH)
        return carry

    lax.fori_loop(1, nz, greet, 0)
    quarter = pl.ds(pl.multiple_of(x * width, 128), width)
    col[y] = jnp.concatenate(
        [tok_ref[:, quarter].astype(F32), cot_ref[:, quarter].astype(F32)], axis=0
    ).astype(BF16)
    rt[y] = router_ref[:, quarter]
    pl.semaphore_wait(barrier, ny - 1 + nx - 1 + 1 + nz - 1)

    for d in range(1, ny):
        there = (y + d) % ny
        rcopy(col.at[y], col.at[y], yt_s.at[d], yt_r.at[d], at_y(there)).start()

    picks = picks_ref[...]
    tokens_here = ny * 8
    ids = lax.broadcasted_iota(jnp.int32, (nz, tokens_here), 0)
    onehot = ((picks[0:1, :] == ids) | (picks[1:2, :] == ids)).astype(F32).astype(BF16)
    t_row = lax.broadcasted_iota(jnp.int32, (tokens_here, lanes), 0)
    q_col = lax.broadcasted_iota(jnp.int32, (tokens_here, lanes), 1)
    t_col = (q_col // 16) * 8 + q_col % 8
    spread = (t_row == t_col).astype(F32).astype(BF16)
    before = (t_row < t_col).astype(F32).astype(BF16)
    onehot_q = jnp.dot(onehot, spread, preferred_element_type=F32)
    prior = jnp.dot(onehot, before, preferred_element_type=F32)
    shape3 = (nz, 16, lanes)
    row = lax.broadcasted_iota(jnp.int32, shape3, 1)
    lane = lax.broadcasted_iota(jnp.int32, shape3, 2)
    same_kind = (row // 8) == ((lane // 8) % 2)
    slot = (row % 8).astype(F32)
    picked = jnp.where(
        same_kind & (jnp.broadcast_to(prior[:, None, :], shape3) == slot),
        jnp.broadcast_to(onehot_q[:, None, :], shape3),
        0.0,
    )
    sel_s[...] = picked

    load_gate.wait()
    load_up.wait()
    load_down.wait()
    for q in range(nx):
        depth = slice(q * width, (q + 1) * width)
        wgu_t[:, depth] = jnp.transpose(wgu[depth, :])
        wd_t[depth, :] = jnp.transpose(wd[:, depth])

    for d in range(1, ny):
        rcopy(col.at[y], col.at[(y + ny - d) % ny], yt_s.at[d], yt_r.at[d], at_y(y)).wait_recv()
    column = col[...].reshape(lanes, width)
    slots[...] = (
        jnp.dot(picked.reshape(nz * 16, lanes).astype(BF16), column, preferred_element_type=F32)
        .astype(BF16)
        .reshape(nz, 16, width)
    )

    def z_forward(p):
        there = (z - offset(p) + nz) % nz
        return rcopy(slots.at[there], xr.at[x, p, core], zf_s.at[p], zf_r.at[p], at_z(there))

    def z_send(p, carry):
        z_forward(p).start()
        return carry

    def z_send_group(g):
        lax.fori_loop(jnp.maximum(g * chunks, 1), (g + 1) * chunks, z_send, 0)

    lax.fori_loop(1, min(window, groups) * chunks, z_send, 0)
    xr[x, 0, core] = slots[z]

    logits = lax.dot_general(rt[y], column, NT, preferred_element_type=F32)
    lg[x] = logits
    for d in range(1, ny):
        rcopy(rt.at[y], rt.at[y], yr_s.at[d], yr_r.at[d], at_y((y + d) % ny)).start()
    for d in range(1, nx):
        rcopy(lg.at[x], lg.at[x], lg_s.at[d], lg_r.at[d], at_x((x + d) % nx)).start()

    def part(g):
        return pl.ds(g * chunks, chunks)

    def to_plane(d, g):
        block = xr.at[x, part(g), core]
        return rcopy(block, block, xa_s.at[g, d], xa_r.at[g, d], at_x((x + d) % nx))

    def from_plane(d, g):
        block = xr.at[(x + nx - d) % nx, part(g), core]
        return rcopy(block, block, xa_s.at[g, d], xa_r.at[g, d], at_x(x))

    def to_partner(q, g):
        block = xr.at[q, part(g), core]
        return rcopy(block, block, pc_s.at[g, q], pc_r.at[g, q], partner)

    def from_partner(q, g):
        block = xr.at[q, part(g), other]
        return rcopy(block, block, pc_s.at[g, q], pc_r.at[g, q], partner)

    def parts_to_partner(g):
        return rcopy(pt.at[:, part(g), other], prcv.at[:, part(g)], pr_s.at[g], pr_r.at[g], partner)

    def pair_sum(q, places):
        return pt[q, places, core].astype(F32) + prcv[q, places].astype(F32)

    def sum_to(d, g):
        there = (x + d) % nx
        return rcopy(sb.at[d, part(g)], rb.at[d, part(g)], rb_s.at[g, d], rb_r.at[g, d], at_x(there))

    def z_back(p):
        there = (z + offset(p) + nz) % nz
        return rcopy(zs.at[p], ret.at[z], zr_s.at[p], zr_r.at[p], at_z(there))

    def stage_arrive(g):
        def wait_one(p, carry):
            z_forward(p).wait_recv()
            return carry

        lax.fori_loop(jnp.maximum(g * chunks, 1), (g + 1) * chunks, wait_one, 0)

        @pl.when(g + window < groups)
        def _():
            z_send_group(g + window)

        for d in (2, 1, 3):
            to_plane(d, g).start()
        to_partner(x, g).start()

    def stage_planes(g):
        for d in (1, 3, 2):
            from_plane(d, g).wait_recv()
            to_partner((x + nx - d) % nx, g).start()

    def stage_compute(g):
        for q in range(nx):
            from_partner(q, g).wait_recv()
        rows = chunks * 2
        gate_up = jnp.zeros((rows * 16, 256), F32)
        grad_hidden = jnp.zeros((rows * 16, 128), F32)
        for q in range(nx):
            block = xr[q, part(g)].reshape(rows * 16, width)
            depth = slice(q * width, (q + 1) * width)
            gate_up = gate_up + jnp.dot(block, wgu[depth, :], preferred_element_type=F32)
            grad_hidden = grad_hidden + jnp.dot(block, wd_t[depth, :], preferred_element_type=F32)
        gate_up = gate_up.reshape(rows, 16, 256)[:, 0:8, :].reshape(rows * 8, 256)
        grad_hidden = grad_hidden.reshape(rows, 16, 128)[:, 8:16, :].reshape(rows * 8, 128)
        gate, up = gate_up[:, 0:128], gate_up[:, 128:256]
        sig = jax.nn.sigmoid(gate)
        act = gate * sig
        hidden = (act * up).astype(BF16)
        both = jnp.concatenate(
            [grad_hidden * up * sig * (1.0 + gate * (1.0 - sig)), grad_hidden * act], axis=1
        ).astype(BF16)
        for q in range(nx):
            depth = slice(q * width, (q + 1) * width)
            out = jnp.dot(hidden, wd[:, depth], preferred_element_type=F32)
            grad = jnp.dot(both, wgu_t[:, depth], preferred_element_type=F32)
            joined = jnp.concatenate(
                [out.reshape(rows, 8, width), grad.reshape(rows, 8, width)], axis=1
            ).astype(BF16)
            pt[q, part(g)] = joined.reshape(chunks, 2, 16, width)
        parts_to_partner(g).start()

    def stage_pair(g):
        parts_to_partner(g).wait_recv()
        for d in (2, 1, 3):
            sb[d, part(g)] = pair_sum((x + d) % nx, part(g)).astype(BF16)
            sum_to(d, g).start()

    def stage_return(g):
        total = pair_sum(x, part(g))
        for d in range(1, nx):
            sum_to(d, g).wait_recv()
            total = total + rb[d, part(g)].astype(F32)
        zs[part(g)] = total.astype(BF16)

        def send_one(p, carry):
            z_back(p).start()
            return carry

        lax.fori_loop(jnp.maximum(g * chunks, 1), (g + 1) * chunks, send_one, 0)

    stages = (
        (stage_arrive, 0), (stage_return, 5), (stage_compute, 2), (stage_pair, 3), (stage_planes, 1),
    )

    def step(it, carry):
        for stage, lag in stages:
            g = it - lag

            @pl.when((g >= 0) & (g < groups))
            def _(stage=stage, g=g):
                stage(g)

        return carry

    lax.fori_loop(0, groups + 5, step, 0)

    for d in range(1, nx):
        rcopy(lg.at[x], lg.at[(x + nx - d) % nx], lg_s.at[d], lg_r.at[d], at_x(x)).wait_recv()
    score = jax.nn.sigmoid((lg[0] + lg[1]) + (lg[2] + lg[3]))
    lane2 = lax.broadcasted_iota(jnp.int32, (nz, lanes), 1)
    token_lane = (lane2 // 8) % 2 == 0
    score = jnp.where(token_lane, score, pltpu.roll(score, 8, 1))
    weighted = sel_s[...] * jnp.broadcast_to(score[:, None, :], shape3)
    weighted = jnp.transpose(weighted.reshape(nz * 16, lanes))
    high = weighted.astype(BF16)
    wt[0] = high
    wt[1] = (weighted - high.astype(F32)).astype(BF16)

    ret[z] = zs[0]

    def wait_back(p, carry):
        there = (z - offset(p) + nz) % nz
        rcopy(zs.at[p], ret.at[there], zr_s.at[p], zr_r.at[p], at_z(z)).wait_recv()
        return carry

    lax.fori_loop(1, nz, wait_back, 0)
    back = ret[...].reshape(nz * 16, width)
    cross = lax.dot_general(back, col[...].reshape(lanes, width), NT, preferred_element_type=F32)
    cross = cross.reshape(shape3)[:, 0:8, :] * sel_s[:, 8:16, :]
    pd[x] = jnp.sum(cross, axis=1)
    for d in range(1, nx):
        rcopy(pd.at[x], pd.at[x], pd_s.at[d], pd_r.at[d], at_x((x + d) % nx)).start()
    mixed = jnp.dot(wt[0], back, preferred_element_type=F32) + jnp.dot(
        wt[1], back, preferred_element_type=F32
    )
    mg[...] = mixed.astype(BF16).reshape(ny, 16, width)
    for d in range(1, ny):
        there = (y + d) % ny
        rcopy(mg.at[there], mgr.at[y], ym_s.at[d], ym_r.at[d], at_y(there)).start()
    mgr[y] = mg[y]
    for d in range(1, nx):
        rcopy(pd.at[x], pd.at[(x + nx - d) % nx], pd_s.at[d], pd_r.at[d], at_x(x)).wait_recv()
    table = jnp.where(token_lane, score * onehot_q, (pd[0] + pd[1]) + (pd[2] + pd[3]))
    table = jnp.concatenate([table, jnp.zeros((128 - nz, lanes), F32)], axis=0)
    st[...] = jnp.transpose(table).reshape(ny, 16, 128)
    for d in range(1, ny):
        there = (y + d) % ny
        rcopy(st.at[there], hs.at[y], ys_s.at[d], ys_r.at[d], at_y(there)).start()
    hs[y] = st[y]

    for d in range(1, ny):
        there = (y + ny - d) % ny
        rcopy(rt.at[there], rt.at[there], yr_s.at[d], yr_r.at[d], at_y(y)).wait_recv()
        rcopy(mg.at[there], mgr.at[there], ym_s.at[d], ym_r.at[d], at_y(y)).wait_recv()
        rcopy(st.at[there], hs.at[there], ys_s.at[d], ys_r.at[d], at_y(y)).wait_recv()
    total = mgr[0].astype(F32)
    terms = hs[0]
    for g in range(1, ny):
        total = total + mgr[g].astype(F32)
        terms = terms + pltpu.roll(hs[g], g * nz, 1)
    s, dots = terms[0:8], terms[8:16]
    slope = s * (1.0 - s)
    dot_slope = slope * dots
    slope_high = slope.astype(BF16).astype(F32)
    dot_high = dot_slope.astype(BF16).astype(F32)
    factors = jnp.concatenate(
        [slope_high, slope - slope_high, dot_high, dot_slope - dot_high], axis=0
    ).astype(BF16)
    experts = ny * nz
    by_router = jnp.dot(
        factors[:, 0:experts], rt[...].reshape(experts, width), preferred_element_type=F32
    )
    slope_sum = by_router[0:8] + by_router[8:16]
    grad_sum = total[8:16] + (by_router[16:24] + by_router[24:32])
    gate_sum = jnp.sum(s, axis=1, keepdims=True)
    dot_sum = jnp.sum(s * dots, axis=1, keepdims=True)
    factor = route_scale / gate_sum
    out_ref[...] = (total[0:8] * factor).astype(BF16)
    grad_ref[...] = (grad_sum * factor - slope_sum * (factor * dot_sum / gate_sum)).astype(BF16)

    for d in range(1, ny):
        rcopy(col.at[y], col.at[y], yt_s.at[d], yt_r.at[d], at_y(y)).wait_send()
        rcopy(rt.at[y], rt.at[y], yr_s.at[d], yr_r.at[d], at_y(y)).wait_send()
        rcopy(mg.at[y], mgr.at[y], ym_s.at[d], ym_r.at[d], at_y(y)).wait_send()
        rcopy(st.at[y], hs.at[y], ys_s.at[d], ys_r.at[d], at_y(y)).wait_send()
    for d in range(1, nx):
        rcopy(lg.at[x], lg.at[x], lg_s.at[d], lg_r.at[d], at_x(x)).wait_send()
        rcopy(pd.at[x], pd.at[x], pd_s.at[d], pd_r.at[d], at_x(x)).wait_send()

    def sent_z(p, carry):
        z_forward(p).wait_send()
        z_back(p).wait_send()
        return carry

    lax.fori_loop(1, nz, sent_z, 0)

    def sent_group(g, carry):
        for d in range(1, nx):
            to_plane(d, g).wait_send()
            sum_to(d, g).wait_send()
        for q in range(nx):
            to_partner(q, g).wait_send()
        parts_to_partner(g).wait_send()
        return carry

    lax.fori_loop(0, groups, sent_group, 0)


def on_device(chunks, window, tokens, cotangent, router, w_gate, w_up, w_down, group_picks):
    ny = lax.axis_size("group")
    nz = lax.axis_size("expert") // 2
    nx = lax.axis_size("rep")
    width = tokens.shape[1] // nx
    groups = nz // chunks
    lanes = ny * 16
    dma = pltpu.SemaphoreType.DMA
    vmem = pl.BlockSpec(memory_space=pltpu.VMEM)
    hbm = pl.BlockSpec(memory_space=pl.ANY)
    result = jax.ShapeDtypeStruct((tokens.shape[0], width), BF16)
    return pl.pallas_call(
        functools.partial(kernel, ny, nz, nx, chunks, window),
        out_shape=(result, result),
        in_specs=[vmem, vmem, vmem, hbm, hbm, hbm, vmem],
        out_specs=(vmem, vmem),
        scratch_shapes=[
            pltpu.VMEM((nx * width, 256), BF16),
            pltpu.VMEM((128, nx * width), BF16),
            pltpu.VMEM((256, nx * width), BF16),
            pltpu.VMEM((nx * width, 128), BF16),
            pltpu.VMEM((ny, 16, width), BF16),
            pltpu.VMEM((ny, nz, width), BF16),
            pltpu.VMEM((nz, 16, width), BF16),
            pltpu.VMEM((nx, nz, 2, 16, width), BF16),
            pltpu.VMEM((nx, nz, 2, 16, width), BF16),
            pltpu.VMEM((nx, nz, 16, width), BF16),
            pltpu.VMEM((nx, nz, 16, width), BF16),
            pltpu.VMEM((nx, nz, 16, width), BF16),
            pltpu.VMEM((nz, 16, width), BF16),
            pltpu.VMEM((nz, 16, width), BF16),
            pltpu.VMEM((ny, 16, width), BF16),
            pltpu.VMEM((ny, 16, width), BF16),
            pltpu.VMEM((ny, 16, 128), F32),
            pltpu.VMEM((ny, 16, 128), F32),
            pltpu.VMEM((nx, nz, lanes), F32),
            pltpu.VMEM((nx, nz, lanes), F32),
            pltpu.VMEM((nz, 16, lanes), F32),
            pltpu.VMEM((2, lanes, nz * 16), BF16),
            dma((3,)),
        ]
        + [dma((ny,))] * 8
        + [dma((nz,))] * 4
        + [dma((nx,))] * 4
        + [dma((groups, nx))] * 4
        + [dma((groups,))] * 2
        + [dma((groups, nx))] * 2,
        compiler_params=pltpu.CompilerParams(
            collective_id=0, has_side_effects=True, vmem_limit_bytes=56 * 1024 * 1024
        ),
        cost_estimate=pl.CostEstimate(
            flops=3 * 1024 * 1024 * 1024, bytes_accessed=4 * 1024 * 1024, transcendentals=32768
        ),
    )(tokens, cotangent, router.T, w_gate, w_up, w_down, group_picks[0, 0].T)


def solution(mesh):
    return jax.shard_map(
        functools.partial(on_device, 2, 8),
        mesh=mesh,
        in_specs=(
            P(("group", "expert"), None),
            P(("group", "expert"), None),
            P(None, "group"),
            P(("group", "expert"), None, "rep"),
            P(("group", "expert"), None, "rep"),
            P(("group", "expert"), "rep", None),
            P("group", "expert", None, None),
        ),
        out_specs=(P(("group", "expert"), "rep"), P(("group", "expert"), "rep")),
        check_vma=False,
    )
```

```python
import functools

import jax
import jax.numpy as jnp
from jax import lax
from jax.experimental import pallas as pl
from jax.experimental.pallas import tpu as pltpu
from jax.sharding import PartitionSpec as P

MESH = pl.DeviceIdType.MESH
F32 = jnp.float32
BF16 = jnp.bfloat16
route_scale = 2.5
NT = (((1,), (1,)), ((), ()))


def rcopy(src, dst, send, recv, device):
    return pltpu.make_async_remote_copy(
        src_ref=src, dst_ref=dst, send_sem=send, recv_sem=recv, device_id=device, device_id_type=MESH
    )


def kernel(
    ny, nz, nx, chunks, window,
    tok_ref, cot_ref, router_ref, wg_ref, wu_ref, wd_ref, picks_ref,
    out_ref, grad_ref,
    wgu, wd, wgu_t, wd_t, col, rt, slots, xr, pt, prcv, sb, rb, zs, ret, mg, mgr, st, hs, lg, pd, sel_s, wt,
    w_sem,
    yt_s, yt_r, yr_s, yr_r, ym_s, ym_r, ys_s, ys_r,
    zf_s, zf_r, zr_s, zr_r,
    lg_s, lg_r, pd_s, pd_r,
    xa_s, xa_r, pc_s, pc_r, pr_s, pr_r, rb_s, rb_r,
):
    y = lax.axis_index("group")
    e = lax.axis_index("expert")
    x = lax.axis_index("rep")
    z = e // 2
    core = e % 2
    other = 1 - core
    width = tok_ref.shape[1] // nx
    groups = nz // chunks
    lanes = ny * 16

    def at_y(i):
        return (i, e, x)

    def at_z(i):
        return (y, i * 2 + core, x)

    def at_x(i):
        return (y, e, i)

    partner = (y, z * 2 + other, x)

    def offset(p):
        g = p // 2
        m = (g + 1) // 2
        sign = 2 * (g % 2) - 1
        return (p % 2) * (-sign * (nz // 2 - m)) + (1 - p % 2) * (sign * m)

    load_gate = pltpu.make_async_copy(wg_ref.at[0], wgu.at[:, 0:128], w_sem.at[0])
    load_up = pltpu.make_async_copy(wu_ref.at[0], wgu.at[:, 128:256], w_sem.at[1])
    load_down = pltpu.make_async_copy(wd_ref.at[0], wd, w_sem.at[2])
    load_gate.start()
    load_up.start()
    load_down.start()

    barrier = pltpu.get_barrier_semaphore()
    for d in range(1, ny):
        pl.semaphore_signal(barrier, inc=1, device_id=at_y((y + d) % ny), device_id_type=MESH)
    for d in range(1, nx):
        pl.semaphore_signal(barrier, inc=1, device_id=at_x((x + d) % nx), device_id_type=MESH)
    pl.semaphore_signal(barrier, inc=1, device_id=partner, device_id_type=MESH)

    def greet(d, carry):
        pl.semaphore_signal(barrier, inc=1, device_id=at_z((z + d) % nz), device_id_type=MESH)
        return carry

    lax.fori_loop(1, nz, greet, 0)
    quarter = pl.ds(pl.multiple_of(x * width, 128), width)
    col[y] = jnp.concatenate(
        [tok_ref[:, quarter].astype(F32), cot_ref[:, quarter].astype(F32)], axis=0
    ).astype(BF16)
    rt[y] = router_ref[:, quarter]
    pl.semaphore_wait(barrier, ny - 1 + nx - 1 + 1 + nz - 1)

    for d in range(1, ny):
        there = (y + d) % ny
        rcopy(col.at[y], col.at[y], yt_s.at[d], yt_r.at[d], at_y(there)).start()

    picks = picks_ref[...]
    tokens_here = ny * 8
    ids = lax.broadcasted_iota(jnp.int32, (nz, tokens_here), 0)
    onehot = ((picks[0:1, :] == ids) | (picks[1:2, :] == ids)).astype(F32).astype(BF16)
    t_row = lax.broadcasted_iota(jnp.int32, (tokens_here, lanes), 0)
    q_col = lax.broadcasted_iota(jnp.int32, (tokens_here, lanes), 1)
    t_col = (q_col // 16) * 8 + q_col % 8
    spread = (t_row == t_col).astype(F32).astype(BF16)
    before = (t_row < t_col).astype(F32).astype(BF16)
    onehot_q = jnp.dot(onehot, spread, preferred_element_type=F32)
    prior = jnp.dot(onehot, before, preferred_element_type=F32)
    shape3 = (nz, 16, lanes)
    row = lax.broadcasted_iota(jnp.int32, shape3, 1)
    lane = lax.broadcasted_iota(jnp.int32, shape3, 2)
    same_kind = (row // 8) == ((lane // 8) % 2)
    slot = (row % 8).astype(F32)
    picked = jnp.where(
        same_kind & (jnp.broadcast_to(prior[:, None, :], shape3) == slot),
        jnp.broadcast_to(onehot_q[:, None, :], shape3),
        0.0,
    )
    sel_s[...] = picked

    load_gate.wait()
    load_up.wait()
    load_down.wait()
    for q in range(nx):
        depth = slice(q * width, (q + 1) * width)
        wgu_t[:, depth] = jnp.transpose(wgu[depth, :])
        wd_t[depth, :] = jnp.transpose(wd[:, depth])

    for d in range(1, ny):
        rcopy(col.at[y], col.at[(y + ny - d) % ny], yt_s.at[d], yt_r.at[d], at_y(y)).wait_recv()
    column = col[...].reshape(lanes, width)
    slots[...] = (
        jnp.dot(picked.reshape(nz * 16, lanes).astype(BF16), column, preferred_element_type=F32)
        .astype(BF16)
        .reshape(nz, 16, width)
    )

    def z_forward(p):
        there = (z - offset(p) + nz) % nz
        return rcopy(slots.at[there], xr.at[x, p, core], zf_s.at[p], zf_r.at[p], at_z(there))

    def z_send(p, carry):
        z_forward(p).start()
        return carry

    def z_send_group(g):
        lax.fori_loop(jnp.maximum(g * chunks, 1), (g + 1) * chunks, z_send, 0)

    lax.fori_loop(1, min(window, groups) * chunks, z_send, 0)
    xr[x, 0, core] = slots[z]

    logits = lax.dot_general(rt[y], column, NT, preferred_element_type=F32)
    lg[x] = logits
    for d in range(1, ny):
        rcopy(rt.at[y], rt.at[y], yr_s.at[d], yr_r.at[d], at_y((y + d) % ny)).start()
    for d in range(1, nx):
        rcopy(lg.at[x], lg.at[x], lg_s.at[d], lg_r.at[d], at_x((x + d) % nx)).start()

    def part(g):
        return pl.ds(g * chunks, chunks)

    def to_plane(d, g):
        block = xr.at[x, part(g), core]
        return rcopy(block, block, xa_s.at[g, d], xa_r.at[g, d], at_x((x + d) % nx))

    def from_plane(d, g):
        block = xr.at[(x + nx - d) % nx, part(g), core]
        return rcopy(block, block, xa_s.at[g, d], xa_r.at[g, d], at_x(x))

    def to_partner(q, g):
        block = xr.at[q, part(g), core]
        return rcopy(block, block, pc_s.at[g, q], pc_r.at[g, q], partner)

    def from_partner(q, g):
        block = xr.at[q, part(g), other]
        return rcopy(block, block, pc_s.at[g, q], pc_r.at[g, q], partner)

    def parts_to_partner(g):
        return rcopy(pt.at[:, part(g), other], prcv.at[:, part(g)], pr_s.at[g], pr_r.at[g], partner)

    def pair_sum(q, places):
        return pt[q, places, core].astype(F32) + prcv[q, places].astype(F32)

    def sum_to(d, g):
        there = (x + d) % nx
        return rcopy(sb.at[d, part(g)], rb.at[d, part(g)], rb_s.at[g, d], rb_r.at[g, d], at_x(there))

    def z_back(p):
        there = (z + offset(p) + nz) % nz
        return rcopy(zs.at[p], ret.at[z], zr_s.at[p], zr_r.at[p], at_z(there))

    def stage_arrive(g):
        def wait_one(p, carry):
            z_forward(p).wait_recv()
            return carry

        lax.fori_loop(jnp.maximum(g * chunks, 1), (g + 1) * chunks, wait_one, 0)

        @pl.when(g + window < groups)
        def _():
            z_send_group(g + window)

        for d in (2, 1, 3):
            to_plane(d, g).start()
        to_partner(x, g).start()

    def stage_planes(g):
        for d in (1, 3, 2):
            from_plane(d, g).wait_recv()
            to_partner((x + nx - d) % nx, g).start()

    def stage_compute(g):
        for q in range(nx):
            from_partner(q, g).wait_recv()
        rows = chunks * 2
        gate_up = jnp.zeros((rows * 16, 256), F32)
        grad_hidden = jnp.zeros((rows * 16, 128), F32)
        for q in range(nx):
            block = xr[q, part(g)].reshape(rows * 16, width)
            depth = slice(q * width, (q + 1) * width)
            gate_up = gate_up + jnp.dot(block, wgu[depth, :], preferred_element_type=F32)
            grad_hidden = grad_hidden + jnp.dot(block, wd_t[depth, :], preferred_element_type=F32)
        gate_up = gate_up.reshape(rows, 16, 256)[:, 0:8, :].reshape(rows * 8, 256)
        grad_hidden = grad_hidden.reshape(rows, 16, 128)[:, 8:16, :].reshape(rows * 8, 128)
        gate, up = gate_up[:, 0:128], gate_up[:, 128:256]
        sig = jax.nn.sigmoid(gate)
        act = gate * sig
        hidden = (act * up).astype(BF16)
        both = jnp.concatenate(
            [grad_hidden * up * sig * (1.0 + gate * (1.0 - sig)), grad_hidden * act], axis=1
        ).astype(BF16)
        for q in range(nx):
            depth = slice(q * width, (q + 1) * width)
            out = jnp.dot(hidden, wd[:, depth], preferred_element_type=F32)
            grad = jnp.dot(both, wgu_t[:, depth], preferred_element_type=F32)
            joined = jnp.concatenate(
                [out.reshape(rows, 8, width), grad.reshape(rows, 8, width)], axis=1
            ).astype(BF16)
            pt[q, part(g)] = joined.reshape(chunks, 2, 16, width)
        parts_to_partner(g).start()

    def stage_pair(g):
        parts_to_partner(g).wait_recv()
        for d in (2, 1, 3):
            sb[d, part(g)] = pair_sum((x + d) % nx, part(g)).astype(BF16)
            sum_to(d, g).start()

    def stage_return(g):
        total = pair_sum(x, part(g))
        for d in range(1, nx):
            sum_to(d, g).wait_recv()
            total = total + rb[d, part(g)].astype(F32)
        zs[part(g)] = total.astype(BF16)

        def send_one(p, carry):
            z_back(p).start()
            return carry

        lax.fori_loop(jnp.maximum(g * chunks, 1), (g + 1) * chunks, send_one, 0)

    stages = (
        (stage_arrive, 0), (stage_return, 4), (stage_compute, 2), (stage_planes, 1), (stage_pair, 2),
    )

    def step(it, carry):
        for stage, lag in stages:
            g = it - lag

            @pl.when((g >= 0) & (g < groups))
            def _(stage=stage, g=g):
                stage(g)

        return carry

    lax.fori_loop(0, groups + 4, step, 0)

    for d in range(1, nx):
        rcopy(lg.at[x], lg.at[(x + nx - d) % nx], lg_s.at[d], lg_r.at[d], at_x(x)).wait_recv()
    score = jax.nn.sigmoid((lg[0] + lg[1]) + (lg[2] + lg[3]))
    lane2 = lax.broadcasted_iota(jnp.int32, (nz, lanes), 1)
    token_lane = (lane2 // 8) % 2 == 0
    score = jnp.where(token_lane, score, pltpu.roll(score, 8, 1))
    weighted = sel_s[...] * jnp.broadcast_to(score[:, None, :], shape3)
    weighted = jnp.transpose(weighted.reshape(nz * 16, lanes))
    high = weighted.astype(BF16)
    wt[0] = high
    wt[1] = (weighted - high.astype(F32)).astype(BF16)

    ret[z] = zs[0]

    def wait_back(p, carry):
        there = (z - offset(p) + nz) % nz
        rcopy(zs.at[p], ret.at[there], zr_s.at[p], zr_r.at[p], at_z(z)).wait_recv()
        return carry

    lax.fori_loop(1, nz, wait_back, 0)
    back = ret[...].reshape(nz * 16, width)
    cross = lax.dot_general(back, col[...].reshape(lanes, width), NT, preferred_element_type=F32)
    cross = cross.reshape(shape3)[:, 0:8, :] * sel_s[:, 8:16, :]
    pd[x] = jnp.sum(cross, axis=1)
    for d in range(1, nx):
        rcopy(pd.at[x], pd.at[x], pd_s.at[d], pd_r.at[d], at_x((x + d) % nx)).start()
    mixed = jnp.dot(wt[0], back, preferred_element_type=F32) + jnp.dot(
        wt[1], back, preferred_element_type=F32
    )
    mg[...] = mixed.astype(BF16).reshape(ny, 16, width)
    for d in range(1, ny):
        there = (y + d) % ny
        rcopy(mg.at[there], mgr.at[y], ym_s.at[d], ym_r.at[d], at_y(there)).start()
    mgr[y] = mg[y]
    for d in range(1, nx):
        rcopy(pd.at[x], pd.at[(x + nx - d) % nx], pd_s.at[d], pd_r.at[d], at_x(x)).wait_recv()
    table = jnp.where(token_lane, score * onehot_q, (pd[0] + pd[1]) + (pd[2] + pd[3]))
    table = jnp.concatenate([table, jnp.zeros((128 - nz, lanes), F32)], axis=0)
    st[...] = jnp.transpose(table).reshape(ny, 16, 128)
    for d in range(1, ny):
        there = (y + d) % ny
        rcopy(st.at[there], hs.at[y], ys_s.at[d], ys_r.at[d], at_y(there)).start()
    hs[y] = st[y]

    for d in range(1, ny):
        there = (y + ny - d) % ny
        rcopy(rt.at[there], rt.at[there], yr_s.at[d], yr_r.at[d], at_y(y)).wait_recv()
        rcopy(mg.at[there], mgr.at[there], ym_s.at[d], ym_r.at[d], at_y(y)).wait_recv()
        rcopy(st.at[there], hs.at[there], ys_s.at[d], ys_r.at[d], at_y(y)).wait_recv()
    total = mgr[0].astype(F32)
    terms = hs[0]
    for g in range(1, ny):
        total = total + mgr[g].astype(F32)
        terms = terms + pltpu.roll(hs[g], g * nz, 1)
    s, dots = terms[0:8], terms[8:16]
    slope = s * (1.0 - s)
    dot_slope = slope * dots
    slope_high = slope.astype(BF16).astype(F32)
    dot_high = dot_slope.astype(BF16).astype(F32)
    factors = jnp.concatenate(
        [slope_high, slope - slope_high, dot_high, dot_slope - dot_high], axis=0
    ).astype(BF16)
    experts = ny * nz
    by_router = jnp.dot(
        factors[:, 0:experts], rt[...].reshape(experts, width), preferred_element_type=F32
    )
    slope_sum = by_router[0:8] + by_router[8:16]
    grad_sum = total[8:16] + (by_router[16:24] + by_router[24:32])
    gate_sum = jnp.sum(s, axis=1, keepdims=True)
    dot_sum = jnp.sum(s * dots, axis=1, keepdims=True)
    factor = route_scale / gate_sum
    out_ref[...] = (total[0:8] * factor).astype(BF16)
    grad_ref[...] = (grad_sum * factor - slope_sum * (factor * dot_sum / gate_sum)).astype(BF16)

    for d in range(1, ny):
        rcopy(col.at[y], col.at[y], yt_s.at[d], yt_r.at[d], at_y(y)).wait_send()
        rcopy(rt.at[y], rt.at[y], yr_s.at[d], yr_r.at[d], at_y(y)).wait_send()
        rcopy(mg.at[y], mgr.at[y], ym_s.at[d], ym_r.at[d], at_y(y)).wait_send()
        rcopy(st.at[y], hs.at[y], ys_s.at[d], ys_r.at[d], at_y(y)).wait_send()
    for d in range(1, nx):
        rcopy(lg.at[x], lg.at[x], lg_s.at[d], lg_r.at[d], at_x(x)).wait_send()
        rcopy(pd.at[x], pd.at[x], pd_s.at[d], pd_r.at[d], at_x(x)).wait_send()

    def sent_z(p, carry):
        z_forward(p).wait_send()
        z_back(p).wait_send()
        return carry

    lax.fori_loop(1, nz, sent_z, 0)

    def sent_group(g, carry):
        for d in range(1, nx):
            to_plane(d, g).wait_send()
            sum_to(d, g).wait_send()
        for q in range(nx):
            to_partner(q, g).wait_send()
        parts_to_partner(g).wait_send()
        return carry

    lax.fori_loop(0, groups, sent_group, 0)


def on_device(chunks, window, tokens, cotangent, router, w_gate, w_up, w_down, group_picks):
    ny = lax.axis_size("group")
    nz = lax.axis_size("expert") // 2
    nx = lax.axis_size("rep")
    width = tokens.shape[1] // nx
    groups = nz // chunks
    lanes = ny * 16
    dma = pltpu.SemaphoreType.DMA
    vmem = pl.BlockSpec(memory_space=pltpu.VMEM)
    hbm = pl.BlockSpec(memory_space=pl.ANY)
    result = jax.ShapeDtypeStruct((tokens.shape[0], width), BF16)
    return pl.pallas_call(
        functools.partial(kernel, ny, nz, nx, chunks, window),
        out_shape=(result, result),
        in_specs=[vmem, vmem, vmem, hbm, hbm, hbm, vmem],
        out_specs=(vmem, vmem),
        scratch_shapes=[
            pltpu.VMEM((nx * width, 256), BF16),
            pltpu.VMEM((128, nx * width), BF16),
            pltpu.VMEM((256, nx * width), BF16),
            pltpu.VMEM((nx * width, 128), BF16),
            pltpu.VMEM((ny, 16, width), BF16),
            pltpu.VMEM((ny, nz, width), BF16),
            pltpu.VMEM((nz, 16, width), BF16),
            pltpu.VMEM((nx, nz, 2, 16, width), BF16),
            pltpu.VMEM((nx, nz, 2, 16, width), BF16),
            pltpu.VMEM((nx, nz, 16, width), BF16),
            pltpu.VMEM((nx, nz, 16, width), BF16),
            pltpu.VMEM((nx, nz, 16, width), BF16),
            pltpu.VMEM((nz, 16, width), BF16),
            pltpu.VMEM((nz, 16, width), BF16),
            pltpu.VMEM((ny, 16, width), BF16),
            pltpu.VMEM((ny, 16, width), BF16),
            pltpu.VMEM((ny, 16, 128), F32),
            pltpu.VMEM((ny, 16, 128), F32),
            pltpu.VMEM((nx, nz, lanes), F32),
            pltpu.VMEM((nx, nz, lanes), F32),
            pltpu.VMEM((nz, 16, lanes), F32),
            pltpu.VMEM((2, lanes, nz * 16), BF16),
            dma((3,)),
        ]
        + [dma((ny,))] * 8
        + [dma((nz,))] * 4
        + [dma((nx,))] * 4
        + [dma((groups, nx))] * 4
        + [dma((groups,))] * 2
        + [dma((groups, nx))] * 2,
        compiler_params=pltpu.CompilerParams(
            collective_id=0, has_side_effects=True, vmem_limit_bytes=56 * 1024 * 1024
        ),
        cost_estimate=pl.CostEstimate(
            flops=3 * 1024 * 1024 * 1024, bytes_accessed=4 * 1024 * 1024, transcendentals=32768
        ),
    )(tokens, cotangent, router.T, w_gate, w_up, w_down, group_picks[0, 0].T)


def solution(mesh):
    return jax.shard_map(
        functools.partial(on_device, 2, 8),
        mesh=mesh,
        in_specs=(
            P(("group", "expert"), None),
            P(("group", "expert"), None),
            P(None, "group"),
            P(("group", "expert"), None, "rep"),
            P(("group", "expert"), None, "rep"),
            P(("group", "expert"), "rep", None),
            P("group", "expert", None, None),
        ),
        out_specs=(P(("group", "expert"), "rep"), P(("group", "expert"), "rep")),
        check_vma=False,
    )
```
